32 devices in a mesh: row: 4 (over y, x), col: 8 (over z, core).
Axes of the slice: x: 2, y: 2, z: 4, core: 2. Of those that a mesh axis runs over, the one named last changes fastest.
Arguments:
- stiff: bfloat16 [128, 384, 4096], P(('row', 'col')), may hold values from -0.75 to 0.75
- modes: bfloat16 [128, 128, 4096], P(('row', 'col')), may hold values from -0.796875 to 0.796875
- brow: int32 [128, 384], P(('row', 'col')), may hold values from 0 to 127
- bcol: int32 [128, 384], P(('row', 'col')), may hold values from 0 to 127
- live: int32 [128], P(('row', 'col')), may hold values from 96 to 384
- couple: bfloat16 [4, 512, 2, 4096], P('row', 'col'), may hold values from -1.796875 to 1.796875
- dest: int32 [4, 512, 2, 1], P('row', 'col'), may hold values from 0 to 31; in each aligned block of 128 rows (0 to 127, 128 to 255, ..., all dimensions but the last counted through in order) at most 8 rows name the same one
- dest_sub: int32 [4, 512, 2], P('row', 'col'), may hold values from 0 to 3
- dest_block: int32 [4, 512, 2], P('row', 'col'), may hold values from 0 to 127
Outputs:
- modal: float32 [128, 4096], P(('row', 'col'))
- interface: float32 [4, 512, 4096], P('row', 'col')
The draws below stay inside these ranges and needn't reach their ends.
Inputs may be any that keep to these rules, and one draw needn't show every extreme that they name: `dest`: among the coupling blocks held by one device, at most 8 name the same destination device, a bound that some block reaches.
All inputs are finite; a program needn't handle non-finite values.
Results may differ from the reference program's by a relative error of at most 0.0029.
Values may be sent and summed in bfloat16 or wider, within the bound.
A program may use at most 256 MiB of HBM per device.

```python
import math
import jax
import jax.numpy as jnp
import numpy as np
from jax import lax

BS = 64
M = 64
SUB_DEV = 4
NBLK = 128
IC_DEV = 64
NNZ_SUB = 384
SUBS = 128
GR = 4
GC = 512
CAP = 8
DEVICES = 32


def with_ends(values, own_key, least, largest):
    longest = values.shape.index(max(values.shape))
    spots = []
    for shift in (0, 1):
        where = [jax.random.randint(jax.random.fold_in(own_key, axis), (), 0, length) for axis, length in enumerate(values.shape)]
        where[longest] = (where[longest] + shift) % values.shape[longest]
        spots.append(tuple(where))
    return values.at[spots[0]].set(least).at[spots[1]].set(largest)


def shard_levels(stream_key, shape, split, smallest, top_value):
    loudness = 1.0
    for axis_at, shards_of in split:
        heights = jax.random.uniform(jax.random.fold_in(jax.random.fold_in(stream_key, 6), axis_at), (shards_of,), jnp.float32, smallest / len(split), top_value / len(split))
        loudness = loudness * jnp.repeat(jnp.exp(heights), shape[axis_at] // shards_of).reshape((-1,) + (1,) * (len(shape) - 1 - axis_at))
    return loudness


def routed_block(key, own, number, rows, number_of, top, reach, lean):
    order = jax.random.permutation(key, number_of)
    crowded, usual = shares(number_of, rows * top, reach, lean, True), shares(number_of, rows * top, reach, lean, False)
    places = jnp.arange(number_of)

    def named(sizes, rotation):
        used = int((sizes > 0).sum())
        fixed = max(1, used // 4)
        shifted = fixed + (places - fixed + rotation * (used - fixed)) % max(1, number_of - fixed)
        return jnp.zeros((number_of,), jnp.int32).at[order[jnp.where(places < fixed, places, shifted)]].set(jnp.asarray(sizes, jnp.int32))

    sizes = jnp.where(number % 4 == 0, named(crowded, number // 4), named(usual, number - number // 4 - 1))
    mixed = jax.random.permutation(jax.random.fold_in(own, 3), number_of)
    giver, receiver = mixed[0:number_of // 2 * 2:2], mixed[1:number_of // 2 * 2:2]
    room = jnp.minimum(sizes[giver] - 1, reach - sizes[receiver]) // 2
    room = jnp.where((giver == order[0]) | (receiver == order[0]) | (sizes[receiver] == 0), 0, jnp.maximum(room, 0))
    shifted = jax.random.randint(jax.random.fold_in(own, 4), (number_of // 2,), 0, 1 << 20) % (room + 1)
    sizes = sizes.at[giver].add(-shifted).at[receiver].add(shifted)
    members = jnp.searchsorted(jnp.cumsum(sizes), jnp.arange(rows * top), side="right").astype(jnp.int32)
    listing = members.reshape(top, rows).T
    listing = listing[jax.random.permutation(jax.random.fold_in(own, 1), rows)]
    rotation = jax.random.randint(jax.random.fold_in(own, 2), (rows, 1), 0, top)
    return jnp.take_along_axis(listing, (jnp.arange(top)[None, :] + rotation) % top, axis=1)


def shares(number_of, total, limit, skew, full):
    portions = [(1 << 20) // math.isqrt(grade ** skew) + 1 for grade in range(1, number_of + 1)]
    largest = limit if full else min(limit, max(-(-total // number_of), total * portions[0] // sum(portions)))
    least = 1 if total - largest >= number_of - 1 else 0
    given, surplus = [largest] + [least] * (number_of - 1), total - largest - least * (number_of - 1)
    while surplus > 0:
        free = [i for i in range(1, number_of) if given[i] < largest] or [i for i in range(1, number_of) if given[i] < limit]
        mass, left = sum([portions[i] for i in free]), surplus
        for i in free:
            extra = min(limit - given[i], max(1, left * portions[i] // mass), surplus)
            given[i] = given[i] + extra
            surplus = surplus - extra
    return np.array(given)


def gaussian(own_key, extent, deviation, reach, shards=(), kind=jnp.bfloat16):
    values = jax.random.normal(own_key, extent, jnp.float32) * deviation
    if len(shards) > 0:
        values = shard_levels(own_key, extent, shards, -0.22, 0.18) * values
    return jnp.clip(values, min=-reach, max=reach).astype(kind)


def setup_inputs(seed: int = 0) -> dict:
    key_list = jax.random.split(jax.random.key(seed), 10)
    stiff = gaussian(key_list[0], (SUBS, NNZ_SUB, BS * BS), BS ** -0.5, 0.75, ((0, 32),))
    modes = gaussian(key_list[1], (SUBS, NBLK, BS * M), 0.1, 0.796875, ((0, 32),))
    brow = with_ends(jax.random.randint(key_list[2], (SUBS, NNZ_SUB), 0, NBLK), jax.random.fold_in(key_list[2], 1), 0, NBLK - 1).astype(jnp.int32)
    bcol = with_ends(jax.random.randint(key_list[3], (SUBS, NNZ_SUB), 0, NBLK), jax.random.fold_in(key_list[3], 1), 0, NBLK - 1).astype(jnp.int32)
    live = with_ends(jax.random.randint(key_list[4], (SUBS,), NNZ_SUB // 4, NNZ_SUB + 1), jax.random.fold_in(key_list[4], 1), NNZ_SUB // 4, NNZ_SUB).astype(jnp.int32)
    couple = gaussian(key_list[5], (GR, GC, 2, BS * BS), 0.3, 1.796875, ((0, 4), (1, 8)))
    dest_keys = jax.random.split(jax.random.fold_in(key_list[6], 1), GR * GC * 2 // (2 * IC_DEV))
    dest_turns = jax.random.permutation(jax.random.fold_in(key_list[6], 3), GR * GC * 2 // (2 * IC_DEV))
    dest = jax.vmap(lambda own, number: routed_block(jax.random.fold_in(key_list[6], 2), own, number, 2 * IC_DEV, DEVICES, 1, CAP, 2))(dest_keys, dest_turns).reshape((GR, GC, 2, 1))
    dest_sub = with_ends(jax.random.randint(key_list[7], (GR, GC, 2), 0, SUB_DEV), jax.random.fold_in(key_list[7], 1), 0, SUB_DEV - 1).astype(jnp.int32)
    dest_block = with_ends(jax.random.randint(key_list[8], (GR, GC, 2), 0, NBLK), jax.random.fold_in(key_list[8], 1), 0, NBLK - 1).astype(jnp.int32)
    return dict(stiff=stiff, modes=modes, brow=brow, bcol=bcol, live=live, couple=couple, dest=dest, dest_sub=dest_sub, dest_block=dest_block)


def one_substructure(items):
    blocks, panel, rows, cols, count = items
    nnz = blocks.shape[0]
    nblk = panel.shape[0]
    kb = blocks.reshape(nnz, BS, BS).astype(jnp.float32)
    pb = panel.reshape(nblk, BS, M).astype(jnp.float32)
    picked = pb[cols]
    term = jnp.einsum("nij,njm->nim", kb, picked)
    keep = (jnp.arange(nnz, dtype=jnp.int32) < count).astype(jnp.float32)
    term = term * keep[:, None, None]
    summed = jax.ops.segment_sum(term, rows, num_segments=nblk)
    applied = summed.astype(jnp.bfloat16).astype(jnp.float32)
    result = jnp.einsum("bim,bin->mn", pb, applied)
    return result.reshape(M * M)


def reference(stiff, modes, brow, bcol, live, couple, dest, dest_sub, dest_block):
    modal = lax.map(one_substructure, (stiff, modes, brow, bcol, live))
    total = modes.shape[0]
    nblk = modes.shape[1]
    panels_all = modes.reshape(total, nblk, BS, M)

    def one_row(items):
        blocks, target, local, block_id = items
        owner = target[:, :, 0] * SUB_DEV + local
        chosen = panels_all[owner, block_id].astype(jnp.float32)
        cb = blocks.reshape(blocks.shape[0], 2, BS, BS).astype(jnp.float32)
        panel = jnp.einsum("gcij,gcjm->gcim", cb, chosen).astype(jnp.bfloat16).astype(jnp.float32)
        tile = jnp.einsum("gcim,gcjm->gij", panel, panel)
        return tile.reshape(blocks.shape[0], BS * BS)

    interface = lax.map(one_row, (couple, dest, dest_sub, dest_block))
    return modal, interface
```

```python
import functools

import jax
import jax.numpy as jnp
from jax import lax
from jax.experimental import pallas as pl
from jax.experimental.pallas import tpu as pltpu
from jax.sharding import PartitionSpec as P

BS = 64
M = 64
LANES = 128
ROWS = BS * M // LANES
CHUNK = 128
GROUP = 32
MIB = 1 << 20


def spread(src_ref, row, count, tmp_ref, base):
    for t in range(ROWS):
        part = src_ref[pl.ds(row, count), t * LANES : (t + 1) * LANES].astype(jnp.float32)
        for h in range(count // 8):
            tmp_ref[pl.ds(base + h * 8 * ROWS + t * 8, 8), :] = part[h * 8 : (h + 1) * 8]


def taken(tmp_ref, base, u):
    return tmp_ref[pl.ds(base + (u // 8) * 8 * ROWS + u % 8, ROWS, stride=8), :]


def low_lanes(rows):
    return lax.broadcasted_iota(jnp.int32, (rows, LANES), 1) < LANES // 2


def doubled(packed, tmp_ref, base):
    turned = pltpu.roll(packed, LANES // 2, 1)
    low = low_lanes(ROWS)
    tmp_ref[pl.ds(base, ROWS, stride=2), :] = jnp.where(low, packed, turned)
    tmp_ref[pl.ds(base + 1, ROWS, stride=2), :] = jnp.where(low, turned, packed)
    return tmp_ref[pl.ds(base, BS), :]


def pack_kernel(modes_ref, out_ref, tmp_ref):
    per = 16
    for g in range(modes_ref.shape[0] // per):
        base = g * per * ROWS
        spread(modes_ref, g * per, per, tmp_ref, base)
        for u in range(per):
            out_ref[g * per + u] = taken(tmp_ref, base, u).astype(jnp.bfloat16)


def pack_modes(modes):
    count = modes.shape[0]
    step = 64
    return pl.pallas_call(
        pack_kernel,
        grid=(count // step,),
        in_specs=[pl.BlockSpec((step, BS * M), lambda i: (i, 0))],
        out_specs=pl.BlockSpec((step, ROWS, LANES), lambda i: (i, 0, 0)),
        out_shape=jax.ShapeDtypeStruct((count, ROWS, LANES), jnp.bfloat16),
        scratch_shapes=[pltpu.VMEM((step * ROWS, LANES), jnp.float32)],
        compiler_params=pltpu.CompilerParams(vmem_limit_bytes=16 * MIB),
        cost_estimate=pl.CostEstimate(flops=0, bytes_accessed=count * 16384, transcendentals=0),
        name="pack_modes",
    )(modes)


def route_kernel(slots, dest_ref, code_ref, table_ref, place_ref, count_ref):
    devices = count_ref.shape[0]

    @pl.loop(0, devices)
    def _(d):
        count_ref[d] = 0

    @pl.loop(0, devices * slots)
    def _(k):
        table_ref[k] = 0

    @pl.loop(0, dest_ref.shape[0])
    def _(k):
        d = dest_ref[k]
        rank = count_ref[d]
        count_ref[d] = rank + 1
        spot = d * slots + rank
        table_ref[spot] = code_ref[k]
        place_ref[k] = spot


def route(dest, code, devices, slots):
    smem = pl.BlockSpec(memory_space=pltpu.SMEM)
    return pl.pallas_call(
        functools.partial(route_kernel, slots),
        in_specs=[smem, smem],
        out_specs=[smem, smem],
        out_shape=[
            jax.ShapeDtypeStruct((devices * slots,), jnp.int32),
            jax.ShapeDtypeStruct(dest.shape, jnp.int32),
        ],
        scratch_shapes=[pltpu.SMEM((devices,), jnp.int32)],
        name="route",
    )(dest, code)


def gather_kernel(ids_ref, packed_ref, out_ref):
    @pl.loop(0, out_ref.shape[0] // 8)
    def _(g):
        for u in range(8):
            out_ref[g * 8 + u] = packed_ref[ids_ref[g * 8 + u]]


def gather_modes(ids, packed):
    vmem = pl.BlockSpec(memory_space=pltpu.VMEM)
    return pl.pallas_call(
        gather_kernel,
        in_specs=[pl.BlockSpec(memory_space=pltpu.SMEM), vmem],
        out_specs=vmem,
        out_shape=jax.ShapeDtypeStruct((ids.shape[0], ROWS, LANES), jnp.bfloat16),
        compiler_params=pltpu.CompilerParams(vmem_limit_bytes=16 * MIB),
        name="gather_modes",
    )(ids, packed)


def modal_kernel(
    brow_ref, bcol_ref, live_ref, stiff_ref, packed_ref, out_ref, flat_ref, twin_ref, weight_ref, sum_ref
):
    s = pl.program_id(0)
    c = pl.program_id(1)
    nblk = packed_ref.shape[1]
    count = live_ref[s]

    @pl.when(c == 0)
    def _():
        low = low_lanes(BS)

        @pl.loop(0, nblk // 8)
        def _(g):
            for u in range(8):
                b = g * 8 + u
                sum_ref[b] = jnp.zeros((ROWS, LANES), jnp.float32)
                both = doubled(packed_ref[0, b].astype(jnp.float32), twin_ref, u * BS)
                weight_ref[b, :BS] = jnp.where(low, both, 0.0).astype(jnp.bfloat16)
                weight_ref[b, BS:] = jnp.where(low, 0.0, both).astype(jnp.bfloat16)

    first = c * CHUNK
    groups = (jnp.clip(count - first, 0, CHUNK) + GROUP - 1) // GROUP

    @pl.loop(0, groups)
    def _(g):
        terms = []
        for h in range(GROUP // 16):
            spread(stiff_ref.at[0], pl.multiple_of(g * GROUP + h * 16, 16), 16, flat_ref, h * 16 * ROWS)
        for u in range(GROUP):
            block = taken(flat_ref, (u // 16) * 16 * ROWS, u % 16).astype(jnp.bfloat16)
            column = bcol_ref[s, first + g * GROUP + u]
            terms.append(jnp.dot(block, weight_ref[column], preferred_element_type=jnp.float32))
        for u in range(GROUP):
            slot = first + g * GROUP + u
            row = jnp.where(slot < count, brow_ref[s, slot], nblk)
            sum_ref[row] += terms[u]

    @pl.when(c == pl.num_programs(1) - 1)
    def _():
        part = 32
        total = jnp.zeros((LANES, LANES), jnp.float32)
        for k in range(nblk // part):
            left = packed_ref[0, k * part : (k + 1) * part].reshape(part * ROWS, LANES)
            right = sum_ref[k * part : (k + 1) * part].astype(jnp.bfloat16).reshape(part * ROWS, LANES)
            total += lax.dot_general(
                left, right, (((0,), (0,)), ((), ())), preferred_element_type=jnp.float32
            )
        out_ref[0] = total[:M, :M] + total[M:, M:]


def modal_stiffness(stiff, packed, brow, bcol, live):
    nsub, nnz, _ = stiff.shape
    nblk = packed.shape[1]

    def stiff_at(s, c, brow_ref, bcol_ref, live_ref):
        return (s, jnp.minimum(c, jnp.maximum(live_ref[s] - 1, 0) // CHUNK), 0)

    return pl.pallas_call(
        modal_kernel,
        grid_spec=pltpu.PrefetchScalarGridSpec(
            num_scalar_prefetch=3,
            grid=(nsub, nnz // CHUNK),
            in_specs=[
                pl.BlockSpec((1, CHUNK, BS * BS), stiff_at),
                pl.BlockSpec((1, nblk, ROWS, LANES), lambda s, c, *_: (s, 0, 0, 0)),
            ],
            out_specs=pl.BlockSpec((1, M, M), lambda s, c, *_: (s, 0, 0)),
            scratch_shapes=[
                pltpu.VMEM((GROUP * ROWS, LANES), jnp.float32),
                pltpu.VMEM((8 * BS, LANES), jnp.float32),
                pltpu.VMEM((nblk, LANES, LANES), jnp.bfloat16),
                pltpu.VMEM((nblk + 1, ROWS, LANES), jnp.float32),
            ],
        ),
        out_shape=jax.ShapeDtypeStruct((nsub, M, M), jnp.float32),
        compiler_params=pltpu.CompilerParams(vmem_limit_bytes=28 * MIB),
        cost_estimate=pl.CostEstimate(
            flops=40_000_000_000, bytes_accessed=nsub * nnz * BS * BS * 2, transcendentals=0
        ),
        name="modal",
    )(brow, bcol, live, stiff, packed)


def tile_kernel(place_ref, couple_ref, got_ref, out_ref, flat_ref, twin_ref, tile_ref):
    low = low_lanes(BS)
    per = 16

    @pl.loop(0, couple_ref.shape[0] // per)
    def _(g):
        spread(couple_ref, pl.multiple_of(g * per, per), per, flat_ref, 0)
        lefts, rights = [], []
        for u in range(per):
            block = taken(flat_ref, 0, u).astype(jnp.bfloat16)
            chosen = got_ref[place_ref[g * per + u]].astype(jnp.float32)
            both = doubled(chosen, twin_ref, u * BS)
            weight = jnp.concatenate(
                [jnp.where(low, both, 0.0), jnp.where(low, 0.0, both)], axis=0
            ).astype(jnp.bfloat16)
            panel = jnp.dot(block, weight, preferred_element_type=jnp.float32)
            panel = panel.astype(jnp.bfloat16)
            lefts.append(panel)
            both = doubled(panel.astype(jnp.float32), twin_ref, (per + u) * BS)
            rights.append(
                jnp.concatenate(
                    [jnp.where(low, both, 0.0), jnp.where(low, 0.0, both)], axis=0
                ).astype(jnp.bfloat16)
            )
        for k in range(per // 2):
            left = jnp.concatenate(lefts[2 * k : 2 * k + 2], axis=1)
            right = jnp.concatenate(rights[2 * k : 2 * k + 2], axis=1)
            tile_ref[k * ROWS : (k + 1) * ROWS, :] = lax.dot_general(
                left, right, (((1,), (1,)), ((), ())), preferred_element_type=jnp.float32
            )
        start = pl.multiple_of(g * (per // 2), per // 2)
        for t in range(ROWS):
            out_ref[pl.ds(start, per // 2), t * LANES : (t + 1) * LANES] = tile_ref[
                pl.ds(t, per // 2, stride=ROWS), :
            ]


def interface_tiles(place, couple, got):
    vmem = pl.BlockSpec(memory_space=pltpu.VMEM)
    tiles = couple.shape[0] // 2
    return pl.pallas_call(
        tile_kernel,
        in_specs=[pl.BlockSpec(memory_space=pltpu.SMEM), vmem, vmem],
        out_specs=vmem,
        out_shape=jax.ShapeDtypeStruct((tiles, BS * BS), jnp.float32),
        scratch_shapes=[
            pltpu.VMEM((16 * ROWS, LANES), jnp.float32),
            pltpu.VMEM((32 * BS, LANES), jnp.float32),
            pltpu.VMEM((8 * ROWS, LANES), jnp.float32),
        ],
        compiler_params=pltpu.CompilerParams(vmem_limit_bytes=24 * MIB),
        name="tiles",
    )(place, couple, got)


def on_device(stiff, modes, brow, bcol, live, couple, dest, dest_sub, dest_block):
    devices = lax.axis_size("row") * lax.axis_size("col")
    nsub, nblk, _ = modes.shape
    couplings = couple.shape[1] * couple.shape[2]
    slots = max(2, 2 * couplings // devices)
    code = dest_sub.reshape(couplings) * nblk + dest_block.reshape(couplings)
    table, place = route(dest.reshape(couplings), code, devices, slots)
    wanted = lax.all_to_all(
        table.reshape(devices, slots), ("row", "col"), split_axis=0, concat_axis=0, tiled=True
    )
    packed = pack_modes(modes.reshape(nsub * nblk, BS * M))
    chosen = gather_modes(wanted.reshape(devices * slots), packed)
    got = lax.all_to_all(
        chosen.reshape(devices, slots * ROWS, LANES),
        ("row", "col"),
        split_axis=0,
        concat_axis=0,
        tiled=True,
    )
    modal = modal_stiffness(stiff, packed.reshape(nsub, nblk, ROWS, LANES), brow, bcol, live)
    tiles = interface_tiles(
        place, couple.reshape(couplings, BS * BS), got.reshape(devices * slots, ROWS, LANES)
    )
    return modal.reshape(nsub, M * M), tiles.reshape(1, couple.shape[1], BS * BS)


def solution(mesh):
    placed = (
        P(("row", "col"), None, None),
        P(("row", "col"), None, None),
        P(("row", "col"), None),
        P(("row", "col"), None),
        P(("row", "col")),
        P("row", "col", None, None),
        P("row", "col", None, None),
        P("row", "col", None),
        P("row", "col", None),
    )
    return jax.shard_map(
        on_device,
        mesh=mesh,
        in_specs=placed,
        out_specs=(P(("row", "col"), None), P("row", "col", None)),
        check_vma=False,
    )
```

```python
import functools

import jax
import jax.numpy as jnp
from jax import lax
from jax.experimental import pallas as pl
from jax.experimental.pallas import tpu as pltpu
from jax.sharding import PartitionSpec as P

BS = 64
M = 64
LANES = 128
ROWS = BS * M // LANES
CHUNK = 128
GROUP = 32
MIB = 1 << 20


def spread(src_ref, row, count, tmp_ref, base):
    for t in range(ROWS):
        part = src_ref[pl.ds(row, count), t * LANES : (t + 1) * LANES].astype(jnp.float32)
        for h in range(count // 8):
            tmp_ref[pl.ds(base + h * 8 * ROWS + t * 8, 8), :] = part[h * 8 : (h + 1) * 8]


def taken(tmp_ref, base, u):
    return tmp_ref[pl.ds(base + (u // 8) * 8 * ROWS + u % 8, ROWS, stride=8), :]


def low_lanes(rows):
    return lax.broadcasted_iota(jnp.int32, (rows, LANES), 1) < LANES // 2


def doubled(packed, tmp_ref, base):
    turned = pltpu.roll(packed, LANES // 2, 1)
    low = low_lanes(ROWS)
    tmp_ref[pl.ds(base, ROWS, stride=2), :] = jnp.where(low, packed, turned)
    tmp_ref[pl.ds(base + 1, ROWS, stride=2), :] = jnp.where(low, turned, packed)
    return tmp_ref[pl.ds(base, BS), :]


def pack_into(modes_ref, packed_ref, tmp_ref, start):
    per = 16
    for g in range(modes_ref.shape[0] // per):
        base = g * per * ROWS
        spread(modes_ref, g * per, per, tmp_ref, base)
        for u in range(per):
            packed_ref[start + g * per + u] = taken(tmp_ref, base, u).astype(jnp.bfloat16)


def route_kernel(nblk, dest_ref, sub_ref, block_ref, table_ref, place_ref, count_ref):
    devices, _, slots = table_ref.shape
    top, length = place_ref.shape

    @pl.loop(0, devices)
    def _(d):
        count_ref[d] = 0
        for k in range(slots):
            table_ref[d, 0, k] = 0

    for c in range(top):

        @pl.loop(0, length, unroll=4)
        def _(k):
            d = dest_ref[c, 0, k]
            rank = count_ref[d]
            count_ref[d] = rank + 1
            table_ref[d, 0, rank] = sub_ref[c, k] * nblk + block_ref[c, k]
            place_ref[c, k] = d * slots + rank


def route(dest, sub, block, nblk, devices, slots):
    smem = pl.BlockSpec(memory_space=pltpu.SMEM)
    return pl.pallas_call(
        functools.partial(route_kernel, nblk),
        in_specs=[smem, smem, smem],
        out_specs=[smem, smem],
        out_shape=[
            jax.ShapeDtypeStruct((devices, 1, slots), jnp.int32),
            jax.ShapeDtypeStruct(sub.shape, jnp.int32),
        ],
        scratch_shapes=[pltpu.SMEM((devices,), jnp.int32)],
        name="route",
    )(dest, sub, block)


def exchange_kernel(
    nrow, ncol, slots, table_ref, modes_ref, packed_ref, out_ref,
    tmp_ref, modes_vmem, packed_vmem, out_vmem, got_ref, ids_ref,
    send_sem, recv_sem, own_sem, in_sem, ids_sem, packed_sem, out_sem,
):
    devices = nrow * ncol
    me = lax.axis_index("row") * ncol + lax.axis_index("col")
    pieces = in_sem.shape[0]
    step = modes_vmem.shape[0] // pieces

    def load(i):
        part = pl.ds(i * step, step)
        return pltpu.make_async_copy(modes_ref.at[part], modes_vmem.at[part], in_sem.at[i])

    for i in range(pieces):
        load(i).start()

    barrier = pltpu.get_barrier_semaphore()

    @pl.loop(1, devices)
    def _(k):
        peer = lax.rem(me + k, devices)
        pl.semaphore_signal(
            barrier, inc=1, device_id=(peer // ncol, lax.rem(peer, ncol)), device_id_type=pl.DeviceIdType.MESH
        )

    own = pltpu.make_async_copy(table_ref.at[me], got_ref.at[me], own_sem)
    own.start()

    def store(i):
        part = pl.ds(i * step, step)
        return pltpu.make_async_copy(packed_vmem.at[part], packed_ref.at[part], packed_sem.at[i])

    def pack(i):
        load(i).wait()
        pack_into(modes_vmem.at[pl.ds(i * step, step)], packed_vmem, tmp_ref, i * step)
        store(i).start()

    early = pieces // 4
    for i in range(early):
        pack(i)

    pl.semaphore_wait(barrier, devices - 1)

    def send(k):
        peer = lax.rem(me + k, devices)
        return pltpu.make_async_remote_copy(
            src_ref=table_ref.at[peer],
            dst_ref=got_ref.at[me],
            send_sem=send_sem.at[k],
            recv_sem=recv_sem.at[me],
            device_id=(peer // ncol, lax.rem(peer, ncol)),
            device_id_type=pl.DeviceIdType.MESH,
        )

    @pl.loop(1, devices)
    def _(k):
        send(k).start()

    for i in range(early, pieces):
        pack(i)

    own.wait()

    @pl.loop(1, devices)
    def _(k):
        source = lax.rem(me + k, devices)
        pltpu.make_async_copy(table_ref.at[source], got_ref.at[source], recv_sem.at[source]).wait()

    @pl.loop(1, devices)
    def _(k):
        send(k).wait_send()

    ids = pltpu.make_async_copy(got_ref, ids_ref, ids_sem)
    ids.start()
    ids.wait()

    @pl.loop(0, devices)
    def _(d):
        for u in range(slots):
            out_vmem[d * slots + u] = packed_vmem[ids_ref[d, 0, u]]

    out = pltpu.make_async_copy(out_vmem, out_ref, out_sem)
    out.start()
    for i in range(pieces):
        store(i).wait()
    out.wait()


def exchange_and_gather(table, modes, nrow, ncol):
    count = modes.shape[0]
    devices, _, slots = table.shape
    wide = jnp.pad(table, ((0, 0), (0, 0), (0, LANES - slots)))
    asked = devices * slots
    pieces = 8
    dma = pltpu.SemaphoreType.DMA
    return pl.pallas_call(
        functools.partial(exchange_kernel, nrow, ncol, slots),
        in_specs=[pl.BlockSpec(memory_space=pltpu.VMEM), pl.BlockSpec(memory_space=pl.ANY)],
        out_specs=[pl.BlockSpec(memory_space=pl.ANY)] * 2,
        out_shape=[
            jax.ShapeDtypeStruct((count, ROWS, LANES), jnp.bfloat16),
            jax.ShapeDtypeStruct((asked, ROWS, LANES), jnp.bfloat16),
        ],
        scratch_shapes=[
            pltpu.VMEM((count // pieces * ROWS, LANES), jnp.float32),
            pltpu.VMEM((count, BS * M), jnp.bfloat16),
            pltpu.VMEM((count, ROWS, LANES), jnp.bfloat16),
            pltpu.VMEM((asked, ROWS, LANES), jnp.bfloat16),
            pltpu.VMEM((devices, 1, LANES), jnp.int32),
            pltpu.SMEM((devices, 1, LANES), jnp.int32),
            dma((devices,)),
            dma((devices,)),
            dma(()),
            dma((pieces,)),
            dma(()),
            dma((pieces,)),
            dma(()),
        ],
        compiler_params=pltpu.CompilerParams(
            vmem_limit_bytes=56 * MIB, collective_id=0, has_side_effects=True
        ),
        name="exchange_and_gather",
    )(wide, modes)


def modal_kernel(
    brow_ref, bcol_ref, live_ref, stiff_ref, packed_ref, out_ref, flat_ref, twin_ref, weight_ref, sum_ref
):
    s = pl.program_id(0)
    c = pl.program_id(1)
    nblk = packed_ref.shape[1]
    count = live_ref[s]

    @pl.when(c == 0)
    def _():
        low = low_lanes(BS)

        @pl.loop(0, nblk // 8)
        def _(g):
            for u in range(8):
                b = g * 8 + u
                sum_ref[b] = jnp.zeros((ROWS, LANES), jnp.float32)
                both = doubled(packed_ref[0, b].astype(jnp.float32), twin_ref, u * BS)
                weight_ref[b, :BS] = jnp.where(low, both, 0.0).astype(jnp.bfloat16)
                weight_ref[b, BS:] = jnp.where(low, 0.0, both).astype(jnp.bfloat16)

    first = c * CHUNK
    groups = (jnp.clip(count - first, 0, CHUNK) + GROUP - 1) // GROUP

    @pl.loop(0, groups)
    def _(g):
        terms = []
        for h in range(GROUP // 16):
            spread(stiff_ref.at[0], pl.multiple_of(g * GROUP + h * 16, 16), 16, flat_ref, h * 16 * ROWS)
        for u in range(GROUP):
            block = taken(flat_ref, (u // 16) * 16 * ROWS, u % 16).astype(jnp.bfloat16)
            column = bcol_ref[s, first + g * GROUP + u]
            terms.append(jnp.dot(block, weight_ref[column], preferred_element_type=jnp.float32))
        for u in range(GROUP):
            slot = first + g * GROUP + u
            row = jnp.where(slot < count, brow_ref[s, slot], nblk)
            sum_ref[row] += terms[u]

    @pl.when(c == pl.num_programs(1) - 1)
    def _():
        part = 32
        total = jnp.zeros((LANES, LANES), jnp.float32)
        for k in range(nblk // part):
            left = packed_ref[0, k * part : (k + 1) * part].reshape(part * ROWS, LANES)
            right = sum_ref[k * part : (k + 1) * part].astype(jnp.bfloat16).reshape(part * ROWS, LANES)
            total += lax.dot_general(
                left, right, (((0,), (0,)), ((), ())), preferred_element_type=jnp.float32
            )
        out_ref[0] = total[:M, :M] + total[M:, M:]


def modal_stiffness(stiff, packed, brow, bcol, live):
    nsub, nnz, _ = stiff.shape
    nblk = packed.shape[1]

    def stiff_at(s, c, brow_ref, bcol_ref, live_ref):
        return (s, jnp.minimum(c, jnp.maximum(live_ref[s] - 1, 0) // CHUNK), 0)

    return pl.pallas_call(
        modal_kernel,
        grid_spec=pltpu.PrefetchScalarGridSpec(
            num_scalar_prefetch=3,
            grid=(nsub, nnz // CHUNK),
            in_specs=[
                pl.BlockSpec((1, CHUNK, BS * BS), stiff_at),
                pl.BlockSpec((1, nblk, ROWS, LANES), lambda s, c, *_: (s, 0, 0, 0)),
            ],
            out_specs=pl.BlockSpec((1, M, M), lambda s, c, *_: (s, 0, 0)),
            scratch_shapes=[
                pltpu.VMEM((GROUP * ROWS, LANES), jnp.float32),
                pltpu.VMEM((8 * BS, LANES), jnp.float32),
                pltpu.VMEM((nblk, LANES, LANES), jnp.bfloat16),
                pltpu.VMEM((nblk + 1, ROWS, LANES), jnp.float32),
            ],
        ),
        out_shape=jax.ShapeDtypeStruct((nsub, M, M), jnp.float32),
        compiler_params=pltpu.CompilerParams(vmem_limit_bytes=28 * MIB),
        cost_estimate=pl.CostEstimate(
            flops=40_000_000_000, bytes_accessed=nsub * nnz * BS * BS * 2, transcendentals=0
        ),
        name="modal",
    )(brow, bcol, live, stiff, packed)


def tile_kernel(place_ref, couple_ref, got_ref, out_ref, flat_ref, twin_ref, tile_ref):
    low = low_lanes(BS)
    per = 16

    @pl.loop(0, couple_ref.shape[0] // per)
    def _(g):
        spread(couple_ref, pl.multiple_of(g * per, per), per, flat_ref, 0)
        lefts, rights = [], []
        for u in range(per):
            block = taken(flat_ref, 0, u).astype(jnp.bfloat16)
            chosen = got_ref[place_ref[u % 2, g * (per // 2) + u // 2]].astype(jnp.float32)
            both = doubled(chosen, twin_ref, u * BS)
            weight = jnp.concatenate(
                [jnp.where(low, both, 0.0), jnp.where(low, 0.0, both)], axis=0
            ).astype(jnp.bfloat16)
            panel = jnp.dot(block, weight, preferred_element_type=jnp.float32)
            panel = panel.astype(jnp.bfloat16)
            lefts.append(panel)
            both = doubled(panel.astype(jnp.float32), twin_ref, (per + u) * BS)
            rights.append(
                jnp.concatenate(
                    [jnp.where(low, both, 0.0), jnp.where(low, 0.0, both)], axis=0
                ).astype(jnp.bfloat16)
            )
        for k in range(per // 2):
            left = jnp.concatenate(lefts[2 * k : 2 * k + 2], axis=1)
            right = jnp.concatenate(rights[2 * k : 2 * k + 2], axis=1)
            tile_ref[k * ROWS : (k + 1) * ROWS, :] = lax.dot_general(
                left, right, (((1,), (1,)), ((), ())), preferred_element_type=jnp.float32
            )
        start = pl.multiple_of(g * (per // 2), per // 2)
        for t in range(ROWS):
            out_ref[pl.ds(start, per // 2), t * LANES : (t + 1) * LANES] = tile_ref[
                pl.ds(t, per // 2, stride=ROWS), :
            ]


def interface_tiles(place, couple, got):
    vmem = pl.BlockSpec(memory_space=pltpu.VMEM)
    tiles = couple.shape[0] // 2
    return pl.pallas_call(
        tile_kernel,
        in_specs=[pl.BlockSpec(memory_space=pltpu.SMEM), vmem, vmem],
        out_specs=vmem,
        out_shape=jax.ShapeDtypeStruct((tiles, BS * BS), jnp.float32),
        scratch_shapes=[
            pltpu.VMEM((16 * ROWS, LANES), jnp.float32),
            pltpu.VMEM((32 * BS, LANES), jnp.float32),
            pltpu.VMEM((8 * ROWS, LANES), jnp.float32),
        ],
        compiler_params=pltpu.CompilerParams(vmem_limit_bytes=24 * MIB),
        name="tiles",
    )(place, couple, got)


def on_device(stiff, modes, brow, bcol, live, couple, dest, dest_sub, dest_block):
    nrow, ncol = lax.axis_size("row"), lax.axis_size("col")
    devices = nrow * ncol
    nsub, nblk, _ = modes.shape
    couplings = couple.shape[1] * couple.shape[2]
    slots = max(2, 2 * couplings // devices)
    table, place = route(
        dest.transpose(2, 0, 3, 1).reshape(couple.shape[2], 1, couple.shape[1]),
        dest_sub[0].T,
        dest_block[0].T,
        nblk,
        devices,
        slots,
    )
    packed, chosen = exchange_and_gather(table, modes.reshape(nsub * nblk, BS * M), nrow, ncol)
    got = lax.all_to_all(
        chosen.reshape(devices, slots * ROWS, LANES),
        ("row", "col"),
        split_axis=0,
        concat_axis=0,
        tiled=True,
    )
    modal = modal_stiffness(stiff, packed.reshape(nsub, nblk, ROWS, LANES), brow, bcol, live)
    tiles = interface_tiles(
        place, couple.reshape(couplings, BS * BS), got.reshape(devices * slots, ROWS, LANES)
    )
    return modal.reshape(nsub, M * M), tiles.reshape(1, couple.shape[1], BS * BS)


def solution(mesh):
    placed = (
        P(("row", "col"), None, None),
        P(("row", "col"), None, None),
        P(("row", "col"), None),
        P(("row", "col"), None),
        P(("row", "col")),
        P("row", "col", None, None),
        P("row", "col", None, None),
        P("row", "col", None),
        P("row", "col", None),
    )
    return jax.shard_map(
        on_device,
        mesh=mesh,
        in_specs=placed,
        out_specs=(P(("row", "col"), None), P("row", "col", None)),
        check_vma=False,
    )
```

```python
import functools

import jax
import jax.numpy as jnp
from jax import lax
from jax.experimental import pallas as pl
from jax.experimental.pallas import tpu as pltpu
from jax.sharding import PartitionSpec as P

BS = 64
M = 64
LANES = 128
ROWS = BS * M // LANES
CHUNK = 128
GROUP = 32
MIB = 1 << 20


def spread(src_ref, row, count, tmp_ref, base):
    for t in range(ROWS):
        part = src_ref[pl.ds(row, count), t * LANES : (t + 1) * LANES].astype(jnp.float32)
        for h in range(count // 8):
            tmp_ref[pl.ds(base + h * 8 * ROWS + t * 8, 8), :] = part[h * 8 : (h + 1) * 8]


def taken(tmp_ref, base, u):
    return tmp_ref[pl.ds(base + (u // 8) * 8 * ROWS + u % 8, ROWS, stride=8), :]


def low_lanes(rows):
    return lax.broadcasted_iota(jnp.int32, (rows, LANES), 1) < LANES // 2


def doubled(packed, tmp_ref, base):
    turned = pltpu.roll(packed, LANES // 2, 1)
    low = low_lanes(ROWS)
    tmp_ref[pl.ds(base, ROWS, stride=2), :] = jnp.where(low, packed, turned)
    tmp_ref[pl.ds(base + 1, ROWS, stride=2), :] = jnp.where(low, turned, packed)
    return tmp_ref[pl.ds(base, BS), :]


def pack_into(modes_ref, packed_ref, tmp_ref, start):
    per = 16
    for g in range(modes_ref.shape[0] // per):
        base = g * per * ROWS
        spread(modes_ref, g * per, per, tmp_ref, base)
        for u in range(per):
            packed_ref[start + g * per + u] = taken(tmp_ref, base, u).astype(jnp.bfloat16)


def route_kernel(nblk, slots, dest_ref, sub_ref, block_ref, table_ref, place_ref, count_ref):
    devices = table_ref.shape[0]
    top, length = place_ref.shape

    @pl.loop(0, devices)
    def _(d):
        count_ref[d] = 0
        for k in range(slots):
            table_ref[d, 0, k] = 0

    for c in range(top):

        @pl.loop(0, length, unroll=4)
        def _(k):
            d = dest_ref[c, 0, k]
            rank = count_ref[d]
            count_ref[d] = rank + 1
            table_ref[d, 0, rank] = sub_ref[c, k] * nblk + block_ref[c, k]
            place_ref[c, k] = d * slots + rank


def route(dest, sub, block, nblk, devices, slots):
    smem = pl.BlockSpec(memory_space=pltpu.SMEM)
    return pl.pallas_call(
        functools.partial(route_kernel, nblk, slots),
        in_specs=[smem, smem, smem],
        out_specs=[smem, smem],
        out_shape=[
            jax.ShapeDtypeStruct((devices, 1, LANES), jnp.int32),
            jax.ShapeDtypeStruct(sub.shape, jnp.int32),
        ],
        scratch_shapes=[pltpu.SMEM((devices,), jnp.int32)],
        name="route",
    )(dest, sub, block)


def exchange_kernel(
    nrow, ncol, slots, table_ref, modes_ref, packed_ref, out_ref,
    tmp_ref, modes_vmem, packed_vmem, out_vmem, got_ref, ids_ref,
    send_sem, recv_sem, own_sem, in_sem, ids_sem, packed_sem, out_sem,
):
    devices = nrow * ncol
    me = lax.axis_index("row") * ncol + lax.axis_index("col")
    pieces = in_sem.shape[0]
    step = modes_vmem.shape[0] // pieces

    def load(i):
        part = pl.ds(i * step, step)
        return pltpu.make_async_copy(modes_ref.at[part], modes_vmem.at[part], in_sem.at[i])

    for i in range(pieces):
        load(i).start()

    barrier = pltpu.get_barrier_semaphore()

    @pl.loop(1, devices)
    def _(k):
        peer = lax.rem(me + k, devices)
        pl.semaphore_signal(
            barrier, inc=1, device_id=(peer // ncol, lax.rem(peer, ncol)), device_id_type=pl.DeviceIdType.MESH
        )

    own = pltpu.make_async_copy(table_ref.at[me], got_ref.at[me], own_sem)
    own.start()

    def store(i):
        part = pl.ds(i * step, step)
        return pltpu.make_async_copy(packed_vmem.at[part], packed_ref.at[part], packed_sem.at[i])

    def pack(i):
        load(i).wait()
        pack_into(modes_vmem.at[pl.ds(i * step, step)], packed_vmem, tmp_ref, i * step)
        store(i).start()

    early = pieces // 4
    for i in range(early):
        pack(i)

    pl.semaphore_wait(barrier, devices - 1)

    def send(k):
        peer = lax.rem(me + k, devices)
        return pltpu.make_async_remote_copy(
            src_ref=table_ref.at[peer],
            dst_ref=got_ref.at[me],
            send_sem=send_sem.at[k],
            recv_sem=recv_sem.at[me],
            device_id=(peer // ncol, lax.rem(peer, ncol)),
            device_id_type=pl.DeviceIdType.MESH,
        )

    @pl.loop(1, devices)
    def _(k):
        send(k).start()

    for i in range(early, pieces):
        pack(i)

    own.wait()

    @pl.loop(1, devices)
    def _(k):
        source = lax.rem(me + k, devices)
        pltpu.make_async_copy(table_ref.at[source], got_ref.at[source], recv_sem.at[source]).wait()

    @pl.loop(1, devices)
    def _(k):
        send(k).wait_send()

    ids = pltpu.make_async_copy(got_ref, ids_ref, ids_sem)
    ids.start()
    ids.wait()

    parts = out_sem.shape[0]
    share = devices // parts

    def leave(i):
        part = pl.ds(i * share * slots, share * slots)
        return pltpu.make_async_copy(out_vmem.at[part], out_ref.at[part], out_sem.at[i])

    for i in range(parts):

        @pl.loop(i * share, (i + 1) * share)
        def _(d):
            for u in range(slots):
                out_vmem[d * slots + u] = packed_vmem[ids_ref[d, 0, u]]

        leave(i).start()

    for i in range(pieces):
        store(i).wait()
    for i in range(parts):
        leave(i).wait()


def exchange_and_gather(table, modes, nrow, ncol, slots):
    count = modes.shape[0]
    devices = table.shape[0]
    asked = devices * slots
    pieces = 8
    dma = pltpu.SemaphoreType.DMA
    return pl.pallas_call(
        functools.partial(exchange_kernel, nrow, ncol, slots),
        in_specs=[pl.BlockSpec(memory_space=pltpu.VMEM), pl.BlockSpec(memory_space=pl.ANY)],
        out_specs=[pl.BlockSpec(memory_space=pl.ANY)] * 2,
        out_shape=[
            jax.ShapeDtypeStruct((count, ROWS, LANES), jnp.bfloat16),
            jax.ShapeDtypeStruct((asked, ROWS, LANES), jnp.bfloat16),
        ],
        scratch_shapes=[
            pltpu.VMEM((count // pieces * ROWS, LANES), jnp.float32),
            pltpu.VMEM((count, BS * M), jnp.bfloat16),
            pltpu.VMEM((count, ROWS, LANES), jnp.bfloat16),
            pltpu.VMEM((asked, ROWS, LANES), jnp.bfloat16),
            pltpu.VMEM((devices, 1, LANES), jnp.int32),
            pltpu.SMEM((devices, 1, LANES), jnp.int32),
            dma((devices,)),
            dma((devices,)),
            dma(()),
            dma((pieces,)),
            dma(()),
            dma((pieces,)),
            dma((4,)),
        ],
        compiler_params=pltpu.CompilerParams(
            vmem_limit_bytes=56 * MIB, collective_id=0, has_side_effects=True
        ),
        name="exchange_and_gather",
    )(table, modes)


def modal_kernel(
    brow_ref, bcol_ref, live_ref, stiff_ref, packed_ref, out_ref, flat_ref, twin_ref, weight_ref, sum_ref
):
    s = pl.program_id(0)
    c = pl.program_id(1)
    nblk = packed_ref.shape[1]
    count = live_ref[s]

    @pl.when(c == 0)
    def _():
        low = low_lanes(BS)

        @pl.loop(0, nblk // 8)
        def _(g):
            for u in range(8):
                b = g * 8 + u
                sum_ref[b] = jnp.zeros((ROWS, LANES), jnp.float32)
                both = doubled(packed_ref[0, b].astype(jnp.float32), twin_ref, u * BS)
                weight_ref[b, :BS] = jnp.where(low, both, 0.0).astype(jnp.bfloat16)
                weight_ref[b, BS:] = jnp.where(low, 0.0, both).astype(jnp.bfloat16)

    first = c * CHUNK
    groups = (jnp.clip(count - first, 0, CHUNK) + GROUP - 1) // GROUP

    @pl.loop(0, groups)
    def _(g):
        terms = []
        for h in range(GROUP // 16):
            spread(stiff_ref.at[0], pl.multiple_of(g * GROUP + h * 16, 16), 16, flat_ref, h * 16 * ROWS)
        for u in range(GROUP):
            block = taken(flat_ref, (u // 16) * 16 * ROWS, u % 16).astype(jnp.bfloat16)
            column = bcol_ref[s, first + g * GROUP + u]
            terms.append(jnp.dot(block, weight_ref[column], preferred_element_type=jnp.float32))
        for u in range(GROUP):
            slot = first + g * GROUP + u
            row = jnp.where(slot < count, brow_ref[s, slot], nblk)
            sum_ref[row] += terms[u]

    @pl.when(c == pl.num_programs(1) - 1)
    def _():
        part = 32
        total = jnp.zeros((LANES, LANES), jnp.float32)
        for k in range(nblk // part):
            left = packed_ref[0, k * part : (k + 1) * part].reshape(part * ROWS, LANES)
            right = sum_ref[k * part : (k + 1) * part].astype(jnp.bfloat16).reshape(part * ROWS, LANES)
            total += lax.dot_general(
                left, right, (((0,), (0,)), ((), ())), preferred_element_type=jnp.float32
            )
        out_ref[0] = total[:M, :M] + total[M:, M:]


def modal_stiffness(stiff, packed, brow, bcol, live):
    nsub, nnz, _ = stiff.shape
    nblk = packed.shape[1]

    def stiff_at(s, c, brow_ref, bcol_ref, live_ref):
        return (s, jnp.minimum(c, jnp.maximum(live_ref[s] - 1, 0) // CHUNK), 0)

    return pl.pallas_call(
        modal_kernel,
        grid_spec=pltpu.PrefetchScalarGridSpec(
            num_scalar_prefetch=3,
            grid=(nsub, nnz // CHUNK),
            in_specs=[
                pl.BlockSpec((1, CHUNK, BS * BS), stiff_at),
                pl.BlockSpec((1, nblk, ROWS, LANES), lambda s, c, *_: (s, 0, 0, 0)),
            ],
            out_specs=pl.BlockSpec((1, M, M), lambda s, c, *_: (s, 0, 0)),
            scratch_shapes=[
                pltpu.VMEM((GROUP * ROWS, LANES), jnp.float32),
                pltpu.VMEM((8 * BS, LANES), jnp.float32),
                pltpu.VMEM((nblk, LANES, LANES), jnp.bfloat16),
                pltpu.VMEM((nblk + 1, ROWS, LANES), jnp.float32),
            ],
        ),
        out_shape=jax.ShapeDtypeStruct((nsub, M, M), jnp.float32),
        compiler_params=pltpu.CompilerParams(vmem_limit_bytes=28 * MIB),
        cost_estimate=pl.CostEstimate(
            flops=40_000_000_000, bytes_accessed=nsub * nnz * BS * BS * 2, transcendentals=0
        ),
        name="modal",
    )(brow, bcol, live, stiff, packed)


def couple_kernel(couple_ref, out_ref, flat_ref):
    per = 16

    @pl.loop(0, couple_ref.shape[0] // per)
    def _(g):
        spread(couple_ref, pl.multiple_of(g * per, per), per, flat_ref, 0)
        for u in range(per):
            out_ref[g * per + u] = taken(flat_ref, 0, u).astype(jnp.bfloat16)


def pack_couple(couple):
    vmem = pl.BlockSpec(memory_space=pltpu.VMEM)
    return pl.pallas_call(
        couple_kernel,
        in_specs=[vmem],
        out_specs=vmem,
        out_shape=jax.ShapeDtypeStruct((couple.shape[0], ROWS, LANES), jnp.bfloat16),
        scratch_shapes=[pltpu.VMEM((16 * ROWS, LANES), jnp.float32)],
        compiler_params=pltpu.CompilerParams(vmem_limit_bytes=16 * MIB),
        cost_estimate=pl.CostEstimate(flops=4_000_000_000, bytes_accessed=3 << 20, transcendentals=0),
        name="pack_couple",
    )(couple)


def tile_kernel(place_ref, couple_ref, got_ref, out_ref, twin_ref, panel_ref, tile_ref):
    low = low_lanes(ROWS)
    tiles = 8

    @pl.loop(0, out_ref.shape[0] // tiles)
    def _(g):
        panels = []
        for u in range(2 * tiles):
            chosen = got_ref[place_ref[u % 2, g * tiles + u // 2]].astype(jnp.float32)
            twin_ref[pl.ds(u * BS, ROWS, stride=2), :] = chosen
            twin_ref[pl.ds(u * BS + 1, ROWS, stride=2), :] = pltpu.roll(chosen, LANES // 2, 1)
        for u in range(2 * tiles):
            block = couple_ref[g * 2 * tiles + u]
            matrix = twin_ref[u * BS : (u + 1) * BS, :].astype(jnp.bfloat16)
            panel = jnp.dot(
                jnp.concatenate([block[:, :BS], block[:, BS:]], axis=0),
                matrix[:, :M],
                preferred_element_type=jnp.float32,
            ).astype(jnp.bfloat16)
            panels.append(panel)
            wide = panel.astype(jnp.float32)
            panel_ref[pl.ds(u * BS, ROWS, stride=2), :M] = wide[:ROWS]
            panel_ref[pl.ds(u * BS + 1, ROWS, stride=2), :M] = wide[ROWS:]
        for k in range(tiles):
            tile = jnp.zeros((BS, LANES), jnp.float32)
            for u in (2 * k, 2 * k + 1):
                ordered = panel_ref[u * BS : (u + 1) * BS, :M].astype(jnp.bfloat16)
                tile += lax.dot_general(
                    panels[u],
                    jnp.concatenate([ordered, ordered], axis=0),
                    (((1,), (1,)), ((), ())),
                    preferred_element_type=jnp.float32,
                )
            tile_ref[k * ROWS : (k + 1) * ROWS, :] = jnp.where(low, tile[:ROWS], tile[ROWS:])
        start = pl.multiple_of(g * tiles, tiles)
        for t in range(ROWS):
            out_ref[pl.ds(start, tiles), t * LANES : (t + 1) * LANES] = tile_ref[
                pl.ds(t, tiles, stride=ROWS), :
            ]


def interface_tiles(place, couple, got):
    vmem = pl.BlockSpec(memory_space=pltpu.VMEM)
    tiles = couple.shape[0] // 2
    return pl.pallas_call(
        tile_kernel,
        in_specs=[pl.BlockSpec(memory_space=pltpu.SMEM), vmem, vmem],
        out_specs=vmem,
        out_shape=jax.ShapeDtypeStruct((tiles, BS * BS), jnp.float32),
        scratch_shapes=[
            pltpu.VMEM((16 * BS, LANES), jnp.float32),
            pltpu.VMEM((16 * BS, LANES), jnp.float32),
            pltpu.VMEM((8 * ROWS, LANES), jnp.float32),
        ],
        compiler_params=pltpu.CompilerParams(vmem_limit_bytes=24 * MIB),
        name="tiles",
    )(place, couple, got)


def on_device(stiff, modes, brow, bcol, live, couple, dest, dest_sub, dest_block):
    nrow, ncol = lax.axis_size("row"), lax.axis_size("col")
    devices = nrow * ncol
    nsub, nblk, _ = modes.shape
    couplings = couple.shape[1] * couple.shape[2]
    slots = max(2, 2 * couplings // devices)
    table, place = route(
        dest.transpose(2, 0, 3, 1).reshape(couple.shape[2], 1, couple.shape[1]),
        dest_sub[0].T,
        dest_block[0].T,
        nblk,
        devices,
        slots,
    )
    packed, chosen = exchange_and_gather(table, modes.reshape(nsub * nblk, BS * M), nrow, ncol, slots)
    got = lax.all_to_all(
        chosen.reshape(devices, slots * ROWS, LANES),
        ("row", "col"),
        split_axis=0,
        concat_axis=0,
        tiled=True,
    )
    modal = modal_stiffness(stiff, packed.reshape(nsub, nblk, ROWS, LANES), brow, bcol, live)
    tiles = interface_tiles(
        place, pack_couple(couple.reshape(couplings, BS * BS)), got.reshape(devices * slots, ROWS, LANES)
    )
    return modal.reshape(nsub, M * M), tiles.reshape(1, couple.shape[1], BS * BS)


def solution(mesh):
    placed = (
        P(("row", "col"), None, None),
        P(("row", "col"), None, None),
        P(("row", "col"), None),
        P(("row", "col"), None),
        P(("row", "col")),
        P("row", "col", None, None),
        P("row", "col", None, None),
        P("row", "col", None),
        P("row", "col", None),
    )
    return jax.shard_map(
        on_device,
        mesh=mesh,
        in_specs=placed,
        out_specs=(P(("row", "col"), None), P("row", "col", None)),
        check_vma=False,
    )
```
